32 devices in a mesh: groups: 2 (over x), train: 16 (over z, y, core).
Axes of the slice: x: 2, y: 2, z: 4, core: 2. Of those that a mesh axis runs over, the one named last changes fastest.
Arguments:
- q_left: bfloat16 [2, 5120, 256], P(None, 'train', 'groups'), parts along dimension 2, may hold values from -6 to 6
- q_right: bfloat16 [2, 5120, 256], P(None, 'train', 'groups'), parts along dimension 2, may hold values from -6 to 6
- left_basis: bfloat16 [2, 5120, 5120], P(None, None, 'train'), may hold values from -0.078125 to 0.078125
- right_basis: bfloat16 [2, 5120, 5120], P(None, None, 'train'), may hold values from -0.078125 to 0.078125
- left_eig: float32 [2, 5120], P(None, 'train'), may hold values from 0.05 to 8
- right_eig: float32 [2, 5120], P(None, 'train'), may hold values from 0.05 to 8
- train_left: bfloat16 [192, 2, 32, 5120], P(('groups', 'train')), parts along dimension 0, may hold values from -0.078125 to 0.078125
- train_right: bfloat16 [192, 2, 32, 5120], P(('groups', 'train')), parts along dimension 0, may hold values from -0.078125 to 0.078125
- seq_ids: int32 [4096], P(('groups', 'train')), parts along dimension 0, may hold values from 0 to 5
Outputs:
- scores: float32 [8, 2048], P('groups', 'train'), parts along dimension 0
The draws below stay inside these ranges and needn't reach their ends.
There are 2 independent parts, one for each index of `groups`. The reference program is written for one: setup_inputs(seed, part) draws one part's arguments, and reference() takes and returns one part's arrays. A program takes and returns all parts, laid end to end along the dimension named above; an argument that names none is the same for every part. Nothing has to cross between parts.
Inputs may be any that keep to these rules, and one draw needn't show every extreme that they name: seq_ids[j] names a row of the table held with entry j, that is of rows (j // 128) * 6 to that plus 6 - 1; rows may repeat.
All inputs are finite; a program needn't handle non-finite values.
Results may differ from the reference program's by a relative error of at most 0.0055.
Values may be sent and summed in bfloat16 or wider, within the bound.
No kernel may reach another device: no remote copies, remote signals or barrier semaphores. Data moves between devices by JAX's collectives and lax.ppermute only.
A program may use at most 128 MiB of HBM per device.

```python
import math
import jax
import jax.numpy as jnp

D = 5120
LAYERS = 2
R = 32
RT = 32
QUERIES = 4
TAB_DEV = 6
SEL_DEV = 128
QR = 128
TABLE = 96
SELECTED = 2048


def plant(entries, stream_key, low, largest):
    index_at = [jax.random.randint(jax.random.fold_in(stream_key, axis), (), 0, length) for axis, length in enumerate(entries.shape)]
    widest = entries.shape.index(max(entries.shape))
    beside = index_at[:widest] + [(index_at[widest] + 1) % entries.shape[widest]] + index_at[widest + 1:]
    return entries.at[tuple(index_at)].set(low).at[tuple(beside)].set(largest)


def block_levels(rng, extent, shards, low, largest):
    def one(position, parts):
        draws = jax.random.uniform(jax.random.fold_in(jax.random.fold_in(rng, 6), position), (parts,), jnp.float32, low / len(shards), largest / len(shards))
        return jnp.repeat(jnp.exp(draws), extent[position] // parts).reshape((-1,) + (1,) * (len(extent) - position - 1))

    gain = one(*shards[0])
    for cut in shards[1:]:
        gain = gain * one(*cut)
    return gain


def noise(own_key, shape, scale, limit, pieces=(), held_as=jnp.bfloat16):
    factor_of = block_levels(own_key, shape, pieces, -0.22, 0.18) if pieces else 1.0
    array = jax.random.normal(own_key, shape, jnp.float32) * scale * factor_of
    return jnp.minimum(jnp.maximum(array, -limit), limit).astype(held_as)


def setup_inputs(seed: int = 0, part: int = 0) -> dict:
    splits = jax.random.split(jax.random.key(seed), 10)
    part_splits = jax.random.split(jax.random.fold_in(splits[9], part), 10)
    return {
        "q_left": noise(part_splits[0], (LAYERS, D, QR), 1.0, 6.0, ((1, 16),)),
        "q_right": noise(part_splits[1], (LAYERS, D, QR), 1.0, 6.0, ((1, 16),)),
        "left_basis": noise(splits[2], (LAYERS, D, D), D ** -0.5, 0.078125, ((2, 16),)),
        "right_basis": noise(splits[3], (LAYERS, D, D), D ** -0.5, 0.078125, ((2, 16),)),
        "left_eig": jnp.clip(jnp.exp(math.log(8.0) - 5.075174 * jax.random.uniform(splits[4], (LAYERS, D), jnp.float32) ** block_levels(splits[4], (LAYERS, D), ((1, 16),), -0.2, 0.2)), 0.05, 8.0),
        "right_eig": jnp.clip(jnp.exp(math.log(8.0) - 5.075174 * jax.random.uniform(splits[5], (LAYERS, D), jnp.float32) ** block_levels(splits[5], (LAYERS, D), ((1, 16),), -0.2, 0.2)), 0.05, 8.0),
        "train_left": noise(part_splits[6], (TABLE, LAYERS, RT, D), D ** -0.5, 0.078125, ((0, 16),)),
        "train_right": noise(part_splits[7], (TABLE, LAYERS, RT, D), D ** -0.5, 0.078125, ((0, 16),)),
        "seq_ids": plant(jax.random.randint(part_splits[8], (SELECTED,), 0, TAB_DEV), jax.random.fold_in(part_splits[8], 1), 0, TAB_DEV - 1).astype(jnp.int32),
    }


DAMP = 0.5


def precondition(factor, basis, eig):
    coeff = jnp.dot(basis.T, factor, preferred_element_type=jnp.float32)
    scaled = (coeff / (eig[:, None] + DAMP)).astype(jnp.bfloat16)
    return jnp.dot(basis, scaled, preferred_element_type=jnp.float32).astype(jnp.bfloat16)


def reference(q_left, q_right, left_basis, right_basis, left_eig, right_eig, train_left, train_right, seq_ids):
    table = train_left.shape[0]
    total = jnp.zeros((QUERIES, table), jnp.float32)
    for layer in range(LAYERS):
        pre_left = precondition(q_left[layer], left_basis[layer], left_eig[layer])
        pre_right = precondition(q_right[layer], right_basis[layer], right_eig[layer])
        proj_left = jnp.einsum("dq,tsd->qts", pre_left.astype(jnp.float32), train_left[:, layer].astype(jnp.float32))
        proj_right = jnp.einsum("dq,tsd->qts", pre_right.astype(jnp.float32), train_right[:, layer].astype(jnp.float32))
        product = (proj_left * proj_right).reshape(QUERIES, R, table, RT)
        total = total + jnp.sum(product, axis=(1, 3))
    shard = jnp.arange(seq_ids.shape[0], dtype=jnp.int32) // SEL_DEV
    rows = (shard * TAB_DEV + seq_ids).astype(jnp.int32)
    return jnp.take(total, rows, axis=1)
```

```python
import functools

import jax
import jax.numpy as jnp
from jax import lax
from jax.experimental import pallas as pl
from jax.experimental.pallas import tpu as pltpu
from jax.sharding import PartitionSpec as P

R = 32
QUERIES = 4
DAMP = 0.5
AXIS = "train"
F32 = jnp.float32
BF16 = jnp.bfloat16


def far_stages(n):
    stages, bit = [], 4
    while bit < n:
        stages.append([bit, 2 * bit, 3 * bit] if 2 * bit < n else [bit])
        bit *= 4
    return stages


def order(n):
    ks = [0]
    for masks in far_stages(n):
        ks = [k ^ m for m in [0] + masks for k in ks]
    return ks


def swap(x, n, mask):
    return lax.ppermute(x, AXIS, [(t, t ^ mask) for t in range(n)])


def gather(own, n):
    block = own
    for masks in far_stages(n):
        block = jnp.concatenate([block] + [swap(block, n, m) for m in masks], axis=0)
    across = swap(block, n, 2)
    return block, across, swap(block, n, 1), swap(across, n, 1)


def scatter_sum(send, keep_near, keep_far, n):
    got = swap(send, n, 1)
    half = keep_near.shape[0]
    across = swap((keep_far + got[half:].astype(F32)).astype(BF16), n, 2)
    total = keep_near + got[:half].astype(F32) + across.astype(F32)
    for masks in reversed(far_stages(n)):
        rows = total.shape[0] // (len(masks) + 1)
        rounded = total.astype(BF16)
        acc = total[:rows]
        for i, m in enumerate(masks, 1):
            acc = acc + swap(rounded[i * rows : (i + 1) * rows], n, m).astype(F32)
        total = acc
    return total.astype(BF16)


def place(me, quarters, full, n):
    rows = full.shape[0] // n
    ks = order(n)
    for quarter, mask in zip(quarters, (0, 2, 1, 3)):
        for i, k in enumerate(ks):
            at = pl.multiple_of((me ^ (k ^ mask)) * rows, rows)
            full[pl.ds(at, rows), :] = quarter[i * rows : (i + 1) * rows, :]


def term_kernel(n, layer, me_ref, qa, qb, qc, qd, basis, eig, send, near, far, full):
    me = me_ref[0]
    place(me, (qa, qb, qc, qd), full, n)
    coeff = lax.dot_general(
        full[...], basis[0], (((0,), (0,)), ((), ())), preferred_element_type=F32
    )
    scaled = (coeff / (eig[layer : layer + 1, :] + DAMP)).astype(BF16)
    rows = full.shape[0] // n
    ks = order(n)
    quarter = len(ks) * rows

    def term(k):
        at = pl.multiple_of((me ^ k) * rows, rows)
        return lax.dot_general(
            basis[0, pl.ds(at, rows), :],
            scaled,
            (((1,), (1,)), ((), ())),
            preferred_element_type=F32,
        )

    for i, k in enumerate(ks):
        at = i * rows
        send[at : at + rows, :] = term(k ^ 1).astype(BF16)
        send[quarter + at : quarter + at + rows, :] = term(k ^ 3).astype(BF16)
        near[at : at + rows, :] = term(k)
        far[at : at + rows, :] = term(k ^ 2)


def terms(me, quarters, basis, eig, layer, n):
    _, width, cols = basis.shape
    q = quarters[0].shape[1]
    whole = lambda a: pl.BlockSpec(a.shape, lambda i, s: (0,) * a.ndim)
    quarter = width // 4
    out = lambda r: pl.BlockSpec((r, q), lambda i, s: (0, 0))
    return pl.pallas_call(
        functools.partial(term_kernel, n, layer),
        grid_spec=pltpu.PrefetchScalarGridSpec(
            num_scalar_prefetch=1,
            grid=(1,),
            in_specs=[whole(a) for a in quarters]
            + [pl.BlockSpec((1, width, cols), lambda i, s: (layer, 0, 0)), whole(eig)],
            out_specs=[out(2 * quarter), out(quarter), out(quarter)],
            scratch_shapes=[pltpu.VMEM((width, q), BF16)],
        ),
        out_shape=[
            jax.ShapeDtypeStruct((2 * quarter, q), BF16),
            jax.ShapeDtypeStruct((quarter, q), F32),
            jax.ShapeDtypeStruct((quarter, q), F32),
        ],
        compiler_params=pltpu.CompilerParams(vmem_limit_bytes=40 * 2**20),
        cost_estimate=pl.CostEstimate(
            flops=4 * width * cols * q, bytes_accessed=2 * width * (cols + 2 * q), transcendentals=0
        ),
        name="terms",
    )(me, *quarters, basis, eig)


def proj_kernel(n, me_ref, pa, pb, pc, pd, train, *rest):
    *other, out, full = rest
    place(me_ref[0], (pa, pb, pc, pd), full, n)
    tables, _, s, width = train.shape
    proj = jnp.dot(
        train[...].reshape(tables * s, width), full[...], preferred_element_type=F32
    )
    if other:
        product = (proj * other[0][...]).reshape(tables, s, proj.shape[1])
        out[...] = jnp.sum(product, axis=1)
    else:
        out[...] = proj


def project(me, quarters, train, layer, n, other=()):
    tables, _, s, width = train.shape
    q = quarters[0].shape[1]
    whole = lambda a: pl.BlockSpec(a.shape, lambda i, r: (0,) * a.ndim)
    shape = (tables, q) if other else (tables * s, q)
    return pl.pallas_call(
        functools.partial(proj_kernel, n),
        grid_spec=pltpu.PrefetchScalarGridSpec(
            num_scalar_prefetch=1,
            grid=(1,),
            in_specs=[whole(a) for a in quarters]
            + [pl.BlockSpec((tables, 1, s, width), lambda i, r: (0, layer, 0, 0))]
            + [whole(a) for a in other],
            out_specs=pl.BlockSpec(shape, lambda i, r: (0, 0)),
            scratch_shapes=[pltpu.VMEM((width, q), BF16)],
        ),
        out_shape=jax.ShapeDtypeStruct(shape, F32),
        compiler_params=pltpu.CompilerParams(vmem_limit_bytes=40 * 2**20),
        cost_estimate=pl.CostEstimate(
            flops=2 * width * tables * s * q,
            bytes_accessed=2 * width * (tables * s + q),
            transcendentals=0,
        ),
        name="project",
    )(me, *quarters, train, *other)


def on_device(
    n, q_left, q_right, left_basis, right_basis, left_eig, right_eig, train_left, train_right, seq_ids
):
    layers = q_left.shape[0]
    tables = train_left.shape[0]
    me = lax.axis_index(AXIS).astype(jnp.int32).reshape(1)
    sides = ((q_left, left_basis, left_eig), (q_right, right_basis, right_eig))
    chunks = [(layer, side) for layer in range(layers) for side in range(2)]
    gathered = {c: gather(sides[c[1]][0][c[0]], n) for c in chunks}
    term = {c: terms(me, gathered[c], sides[c[1]][1], sides[c[1]][2], c[0], n) for c in chunks}
    precond = {c: gather(scatter_sum(*term[c], n), n) for c in chunks}
    total = 0.0
    for layer in range(layers):
        left = project(me, precond[layer, 0], train_left, layer, n)
        total = total + project(me, precond[layer, 1], train_right, layer, n, (left,))
    table_scores = jnp.sum(total.reshape(tables, QUERIES, R), axis=2).T
    match = (seq_ids[None, :] == jnp.arange(tables, dtype=jnp.int32)[:, None]).astype(F32)
    return jnp.dot(table_scores, match, precision=lax.Precision.HIGHEST, preferred_element_type=F32)


def solution(mesh):
    placed = (
        P(None, "train", "groups"),
        P(None, "train", "groups"),
        P(None, None, "train"),
        P(None, None, "train"),
        P(None, "train"),
        P(None, "train"),
        P(("groups", "train"), None, None, None),
        P(("groups", "train"), None, None, None),
        P(("groups", "train")),
    )
    return jax.shard_map(
        functools.partial(on_device, mesh.shape[AXIS]),
        mesh=mesh,
        in_specs=placed,
        out_specs=P("groups", "train"),
        check_vma=False,
    )
```

```python
import functools

import jax
import jax.numpy as jnp
from jax import lax
from jax.experimental import pallas as pl
from jax.experimental.pallas import tpu as pltpu
from jax.sharding import PartitionSpec as P

R = 32
QUERIES = 4
DAMP = 0.5
TOGETHER = 2
SPREAD = 2
PIECES = 4
TERMS_VMEM = 20 * 2**20
AXIS = "train"
F32 = jnp.float32
BF16 = jnp.bfloat16


def far_stages(n, most):
    stages, bit = [], 4
    while bit < n:
        bits = min(most, (n // bit).bit_length() - 1)
        stages.append((bit, bits))
        bit <<= bits
    return stages


def swap(x, n, mask):
    return lax.ppermute(x, AXIS, [(t, t ^ mask) for t in range(n)])


def spread(block, n):
    ks = [0]
    for bit, bits in far_stages(n, SPREAD):
        masks = [bit * j for j in range(1, 1 << bits)]
        block = jnp.concatenate([block] + [swap(block, n, m) for m in masks], axis=1)
        ks = [k ^ m for m in [0] + masks for k in ks]
    return block, ks


def fold(total, me, n):
    result = total.astype(BF16)
    for bit, bits in far_stages(n, 2):
        if bits == 1:
            total = total + swap(result, n, bit).astype(F32)
            result = total.astype(BF16)
            continue
        place = lambda t: (t // bit) % 4
        inward = [(t, t ^ bit) for t in range(n) if place(t) in (0, 3)]
        outward = [(b, a) for a, b in inward]
        middle = [(t, t ^ (3 * bit)) for t in range(n) if place(t) in (1, 2)]
        total = total + lax.ppermute(result, AXIS, inward).astype(F32)
        total = total + lax.ppermute(total.astype(BF16), AXIS, middle).astype(F32)
        result = total.astype(BF16)
        inner = (place(me) == 1) | (place(me) == 2)
        result = jnp.where(inner, result, lax.ppermute(result, AXIS, outward))
        total = result.astype(F32)
    return result


def after(x, earlier):
    return lax.optimization_barrier((x, earlier))[0] if earlier else x


def gather_near(block, n):
    across = swap(block, n, 2)
    return block, across, swap(block, n, 1), swap(across, n, 1)


def term_kernel(n, column, first, offsets, me_ref, *refs):
    *arrays, basis, eig, send, keep, full, held, pair, sems = refs
    me = me_ref[0]
    layers, _, width = held.shape
    rows = width // n
    piece = width // PIECES
    copies = {}
    for l in range(layers):
        for p in range(PIECES):
            part = (slice(None), pl.ds(p * piece, piece))
            copies[l, p] = pltpu.make_async_copy(
                basis.at[first + l].at[part], held.at[l].at[part], sems.at[l, p]
            )
            copies[l, p].start()
    mine = me & 1
    above = (me >> 1) & 1
    for l in range(layers):
        for array, ks in zip(arrays, offsets):
            for i, k in enumerate(ks):
                at = pl.multiple_of((me ^ k) * rows, rows)
                full[pl.ds(at, rows), :] = array[l, i * rows : (i + 1) * rows, :]
        coeff = [0.0, 0.0]
        split = held.shape[1] // 2
        for p in range(PIECES):
            copies[l, p].wait()
            for h in range(2):
                coeff[h] = coeff[h] + jnp.dot(
                    held[l, h * split : (h + 1) * split, p * piece : (p + 1) * piece],
                    full[p * piece : (p + 1) * piece, :],
                    preferred_element_type=F32,
                )
        coeff = jnp.concatenate(coeff, axis=0)
        scale = eig[:, column + l : column + l + 1] + DAMP
        scaled = (coeff / scale).astype(BF16).T
        term = jnp.dot(scaled, held[l], preferred_element_type=F32)
        for p in range(n // 2):
            pair[...] = term[:, 2 * p * rows : 2 * (p + 1) * rows].T
            at = pl.multiple_of(((above ^ (p & 1)) * (n // 4) + p // 2) * rows, rows)
            kept = pl.multiple_of(mine * rows, rows)
            sent = pl.multiple_of((1 - mine) * rows, rows)
            keep[l, pl.ds(at, rows), :] = pair[pl.ds(kept, rows), :]
            send[l, pl.ds(at, rows), :] = pair[pl.ds(sent, rows), :].astype(BF16)


def terms(me, arrays, offsets, basis, eig, first, column, n):
    _, cols, width = basis.shape
    layers, _, q = arrays[0].shape
    vmem = pl.BlockSpec(memory_space=pltpu.VMEM)
    half = (layers, width // 2, q)
    return pl.pallas_call(
        functools.partial(term_kernel, n, column, first, offsets),
        in_specs=[pl.BlockSpec(memory_space=pltpu.SMEM)]
        + [vmem] * len(arrays)
        + [pl.BlockSpec(memory_space=pltpu.HBM), vmem],
        out_specs=[vmem, vmem],
        scratch_shapes=[
            pltpu.VMEM((width, q), BF16),
            pltpu.VMEM((layers, cols, width), BF16),
            pltpu.VMEM((2 * width // n, q), F32),
            pltpu.SemaphoreType.DMA((layers, PIECES)),
        ],
        out_shape=[jax.ShapeDtypeStruct(half, BF16), jax.ShapeDtypeStruct(half, F32)],
        compiler_params=pltpu.CompilerParams(vmem_limit_bytes=TERMS_VMEM),
        cost_estimate=pl.CostEstimate(
            flops=layers * 4 * width * cols * q,
            bytes_accessed=layers * 2 * width * (cols + 2 * q),
            transcendentals=0,
        ),
        name="terms",
    )(me, *arrays, pltpu.with_memory_space_constraint(basis, pltpu.HBM), eig)


def proj_kernel(n, first, me_ref, pa, pb, pc, pd, train, *rest):
    *other, out, full, held, sems = rest
    layers, tables, s, width = held.shape
    rows = width // n
    copies = []
    for l in range(layers):
        copies.append(pltpu.make_async_copy(train.at[:, first + l], held.at[l], sems.at[l]))
        copies[l].start()
    total = 0.0
    for l in range(layers):
        for quarter, mask in zip((pa, pb, pc, pd), (0, 2, 1, 3)):
            for i in range(n // 4):
                at = pl.multiple_of((4 * i + ((me_ref[0] & 3) ^ mask)) * rows, rows)
                full[pl.ds(at, rows), :] = quarter[l, i * rows : (i + 1) * rows, :]
        copies[l].wait()
        proj = jnp.dot(
            held[l].reshape(tables * s, width), full[...], preferred_element_type=F32
        )
        if other:
            product = (proj * other[0][l]).reshape(tables, s, proj.shape[1])
            total = total + jnp.sum(product, axis=1)
        else:
            out[l] = proj
    if other:
        out[...] = total


def project(me, quarters, train, first, n, other=()):
    tables, _, s, width = train.shape
    layers, _, q = quarters[0].shape
    vmem = pl.BlockSpec(memory_space=pltpu.VMEM)
    shape = (tables, q) if other else (layers, tables * s, q)
    return pl.pallas_call(
        functools.partial(proj_kernel, n, first),
        in_specs=[pl.BlockSpec(memory_space=pltpu.SMEM)]
        + [vmem] * 4
        + [pl.BlockSpec(memory_space=pltpu.HBM)]
        + [vmem] * len(other),
        out_specs=vmem,
        scratch_shapes=[
            pltpu.VMEM((width, q), BF16),
            pltpu.VMEM((layers, tables, s, width), BF16),
            pltpu.SemaphoreType.DMA((layers,)),
        ],
        out_shape=jax.ShapeDtypeStruct(shape, F32),
        compiler_params=pltpu.CompilerParams(vmem_limit_bytes=TERMS_VMEM),
        cost_estimate=pl.CostEstimate(
            flops=layers * 2 * width * tables * s * q,
            bytes_accessed=layers * 2 * width * (tables * s + q),
            transcendentals=0,
        ),
        name="project",
    )(me, *quarters, train, *other)


def on_device(
    n, q_left, q_right, left_basis, right_basis, left_eig, right_eig, train_left, train_right, seq_ids
):
    layers = q_left.shape[0]
    tables = train_left.shape[0]
    me = lax.axis_index(AXIS).astype(jnp.int32).reshape(1)
    eig = jnp.concatenate((left_eig, right_eig), axis=0).T
    sides = (
        (q_left, jnp.swapaxes(left_basis, 1, 2), train_left),
        (q_right, jnp.swapaxes(right_basis, 1, 2), train_right),
    )
    chunks = [(first, side) for first in range(0, layers, TOGETHER) for side in range(2)]
    blocks = [spread(sides[side][0][first : first + TOGETHER], n) for first, side in chunks]
    gathered = [gather_near(block, n) for block, _ in blocks]
    aways, halves, quarters = [], [], []
    for i, (first, side) in enumerate(chunks):
        ks = blocks[i][1]
        offsets = [[k ^ m for k in ks] for m in (0, 2, 1, 3)]
        earlier = []
        arrays = after(gathered[i], earlier)
        send, keep = terms(me, arrays, offsets, sides[side][1], eig, first, side * layers + first, n)
        half = keep + swap(send, n, 1).astype(F32)
        quarter = half.shape[1] // 2
        aways.append(half[:, quarter:].astype(BF16))
        halves.append(half[:, :quarter] + swap(aways[i], n, 2).astype(F32))
    total, left = 0.0, ()
    for i, (first, side) in enumerate(chunks):
        precond = gather_near(fold(halves[i], me[0], n), n)
        left = (project(me, precond, sides[side][2], first, n, left),)
        if side:
            total, left = total + left[0], ()
    table_scores = jnp.sum(total.reshape(tables, QUERIES, R), axis=2).T
    match = (seq_ids[None, :] == jnp.arange(tables, dtype=jnp.int32)[:, None]).astype(F32)
    return jnp.dot(table_scores, match, precision=lax.Precision.HIGHEST, preferred_element_type=F32)


def solution(mesh):
    placed = (
        P(None, "train", "groups"),
        P(None, "train", "groups"),
        P(None, None, "train"),
        P(None, None, "train"),
        P(None, "train"),
        P(None, "train"),
        P(("groups", "train"), None, None, None),
        P(("groups", "train"), None, None, None),
        P(("groups", "train")),
    )
    return jax.shard_map(
        functools.partial(on_device, mesh.shape[AXIS]),
        mesh=mesh,
        in_specs=placed,
        out_specs=P("groups", "train"),
        check_vma=False,
    )
```

```python
import functools

import jax
import jax.numpy as jnp
from jax import lax
from jax.experimental import pallas as pl
from jax.experimental.pallas import tpu as pltpu
from jax.sharding import PartitionSpec as P

R = 32
QUERIES = 4
DAMP = 0.5
TOGETHER = 2
SPREAD = 2
PIECES = 4
TERMS_VMEM = 20 * 2**20
AXIS = "train"
F32 = jnp.float32
BF16 = jnp.bfloat16


def far_stages(n, most):
    stages, bit = [], 4
    while bit < n:
        bits = min(most, (n // bit).bit_length() - 1)
        stages.append((bit, bits))
        bit <<= bits
    return stages


def swap(x, n, mask):
    return lax.ppermute(x, AXIS, [(t, t ^ mask) for t in range(n)])


def spread(block, n):
    ks = [0]
    for bit, bits in far_stages(n, SPREAD):
        masks = [bit * j for j in range(1, 1 << bits)]
        block = jnp.concatenate([block] + [swap(block, n, m) for m in masks], axis=1)
        ks = [k ^ m for m in [0] + masks for k in ks]
    return block, ks


def sum_far(total, me, n):
    result = total.astype(BF16)
    for bit, bits in far_stages(n, 2):
        if bits == 1:
            total = total + swap(result, n, bit).astype(F32)
            result = total.astype(BF16)
            continue
        place = (me // bit) % 4
        first = (place == 0) | (place == 3)
        half = total.shape[1] // 2
        low, high = total[:, :half], total[:, half:]
        mine = jnp.where(first, low, high)
        theirs = jnp.where(first, high, low).astype(BF16)
        mine = mine + swap(theirs, n, bit).astype(F32)
        mine = mine + swap(mine.astype(BF16), n, 3 * bit).astype(F32)
        mine = mine.astype(BF16)
        theirs = swap(mine, n, bit)
        result = jnp.concatenate(
            [jnp.where(first, mine, theirs), jnp.where(first, theirs, mine)], axis=1
        )
        total = result.astype(F32)
    return result


def after(x, earlier):
    return lax.optimization_barrier((x, earlier))[0] if earlier else x


def gather_near(block, n):
    across = swap(block, n, 2)
    return block, across, swap(block, n, 1), swap(across, n, 1)


def term_kernel(n, column, first, offsets, me_ref, *refs):
    *arrays, basis, eig, send, keep, full, held, pair, sems = refs
    me = me_ref[0]
    layers, _, width = held.shape
    rows = width // n
    piece = width // PIECES
    copies = {}
    for l in range(layers):
        for p in range(PIECES):
            part = (slice(None), pl.ds(p * piece, piece))
            copies[l, p] = pltpu.make_async_copy(
                basis.at[first + l].at[part], held.at[l].at[part], sems.at[l, p]
            )
            copies[l, p].start()
    mine = me & 1
    above = (me >> 1) & 1
    for l in range(layers):
        for array, ks in zip(arrays, offsets):
            for i, k in enumerate(ks):
                at = pl.multiple_of((me ^ k) * rows, rows)
                full[pl.ds(at, rows), :] = array[l, i * rows : (i + 1) * rows, :]
        coeff = [0.0, 0.0]
        split = held.shape[1] // 2
        for p in range(PIECES):
            copies[l, p].wait()
            for h in range(2):
                coeff[h] = coeff[h] + jnp.dot(
                    held[l, h * split : (h + 1) * split, p * piece : (p + 1) * piece],
                    full[p * piece : (p + 1) * piece, :],
                    preferred_element_type=F32,
                )
        coeff = jnp.concatenate(coeff, axis=0)
        scale = eig[:, column + l : column + l + 1] + DAMP
        scaled = (coeff / scale).astype(BF16).T
        term = jnp.dot(scaled, held[l], preferred_element_type=F32)
        for p in range(n // 2):
            pair[...] = term[:, 2 * p * rows : 2 * (p + 1) * rows].T
            at = pl.multiple_of(((above ^ (p & 1)) * (n // 4) + p // 2) * rows, rows)
            kept = pl.multiple_of(mine * rows, rows)
            sent = pl.multiple_of((1 - mine) * rows, rows)
            keep[l, pl.ds(at, rows), :] = pair[pl.ds(kept, rows), :]
            send[l, pl.ds(at, rows), :] = pair[pl.ds(sent, rows), :].astype(BF16)


def terms(me, arrays, offsets, basis, eig, first, column, n):
    _, cols, width = basis.shape
    layers, _, q = arrays[0].shape
    vmem = pl.BlockSpec(memory_space=pltpu.VMEM)
    half = (layers, width // 2, q)
    return pl.pallas_call(
        functools.partial(term_kernel, n, column, first, offsets),
        in_specs=[pl.BlockSpec(memory_space=pltpu.SMEM)]
        + [vmem] * len(arrays)
        + [pl.BlockSpec(memory_space=pltpu.HBM), vmem],
        out_specs=[vmem, vmem],
        scratch_shapes=[
            pltpu.VMEM((width, q), BF16),
            pltpu.VMEM((layers, cols, width), BF16),
            pltpu.VMEM((2 * width // n, q), F32),
            pltpu.SemaphoreType.DMA((layers, PIECES)),
        ],
        out_shape=[jax.ShapeDtypeStruct(half, BF16), jax.ShapeDtypeStruct(half, F32)],
        compiler_params=pltpu.CompilerParams(vmem_limit_bytes=TERMS_VMEM),
        cost_estimate=pl.CostEstimate(
            flops=layers * 4 * width * cols * q,
            bytes_accessed=layers * 2 * width * (cols + 2 * q),
            transcendentals=0,
        ),
        name="terms",
    )(me, *arrays, pltpu.with_memory_space_constraint(basis, pltpu.HBM), eig)


def proj_kernel(n, first, me_ref, pa, pb, pc, pd, train, *rest):
    *other, out, full, held, sems = rest
    layers, tables, s, width = held.shape
    rows = width // n
    copies = []
    for l in range(layers):
        copies.append(pltpu.make_async_copy(train.at[:, first + l], held.at[l], sems.at[l]))
        copies[l].start()
    total = 0.0
    for l in range(layers):
        for quarter, mask in zip((pa, pb, pc, pd), (0, 2, 1, 3)):
            for i in range(n // 4):
                at = pl.multiple_of((4 * i + ((me_ref[0] & 3) ^ mask)) * rows, rows)
                full[pl.ds(at, rows), :] = quarter[l, i * rows : (i + 1) * rows, :]
        copies[l].wait()
        proj = jnp.dot(
            held[l].reshape(tables * s, width), full[...], preferred_element_type=F32
        )
        if other:
            product = (proj * other[0][l]).reshape(tables, s, proj.shape[1])
            total = total + jnp.sum(product, axis=1)
        else:
            out[l] = proj
    if other:
        out[...] = total


def project(me, quarters, train, first, n, other=()):
    tables, _, s, width = train.shape
    layers, _, q = quarters[0].shape
    vmem = pl.BlockSpec(memory_space=pltpu.VMEM)
    shape = (tables, q) if other else (layers, tables * s, q)
    return pl.pallas_call(
        functools.partial(proj_kernel, n, first),
        in_specs=[pl.BlockSpec(memory_space=pltpu.SMEM)]
        + [vmem] * 4
        + [pl.BlockSpec(memory_space=pltpu.HBM)]
        + [vmem] * len(other),
        out_specs=vmem,
        scratch_shapes=[
            pltpu.VMEM((width, q), BF16),
            pltpu.VMEM((layers, tables, s, width), BF16),
            pltpu.SemaphoreType.DMA((layers,)),
        ],
        out_shape=jax.ShapeDtypeStruct(shape, F32),
        compiler_params=pltpu.CompilerParams(vmem_limit_bytes=TERMS_VMEM),
        cost_estimate=pl.CostEstimate(
            flops=layers * 2 * width * tables * s * q,
            bytes_accessed=layers * 2 * width * (tables * s + q),
            transcendentals=0,
        ),
        name="project",
    )(me, *quarters, train, *other)


def on_device(
    n, q_left, q_right, left_basis, right_basis, left_eig, right_eig, train_left, train_right, seq_ids
):
    layers = q_left.shape[0]
    tables = train_left.shape[0]
    me = lax.axis_index(AXIS).astype(jnp.int32).reshape(1)
    eig = jnp.concatenate((left_eig, right_eig), axis=0).T
    sides = (
        (q_left, jnp.swapaxes(left_basis, 1, 2), train_left),
        (q_right, jnp.swapaxes(right_basis, 1, 2), train_right),
    )
    chunks = [(first, side) for first in range(0, layers, TOGETHER) for side in range(2)]
    blocks = [spread(sides[side][0][first : first + TOGETHER], n) for first, side in chunks]
    gathered = [gather_near(block, n) for block, _ in blocks]
    aways, halves, quarters = [], [], []
    for i, (first, side) in enumerate(chunks):
        ks = blocks[i][1]
        offsets = [[k ^ m for k in ks] for m in (0, 2, 1, 3)]
        earlier = []
        arrays = after(gathered[i], earlier)
        send, keep = terms(me, arrays, offsets, sides[side][1], eig, first, side * layers + first, n)
        half = keep + swap(send, n, 1).astype(F32)
        quarter = half.shape[1] // 2
        aways.append(half[:, quarter:].astype(BF16))
        halves.append(half[:, :quarter] + swap(aways[i], n, 2).astype(F32))
    total, left = 0.0, ()
    for i, (first, side) in enumerate(chunks):
        block = sum_far(halves[i], me[0], n)
        across = swap(block, n, 2)
        corner = swap(after(across, left), n, 1)
        left = (project(me, (block, across, swap(block, n, 1), corner), sides[side][2], first, n, left),)
        if side:
            total, left = total + left[0], ()
    table_scores = jnp.sum(total.reshape(tables, QUERIES, R), axis=2).T
    match = (seq_ids[None, :] == jnp.arange(tables, dtype=jnp.int32)[:, None]).astype(F32)
    return jnp.dot(table_scores, match, precision=lax.Precision.HIGHEST, preferred_element_type=F32)


def solution(mesh):
    placed = (
        P(None, "train", "groups"),
        P(None, "train", "groups"),
        P(None, None, "train"),
        P(None, None, "train"),
        P(None, "train"),
        P(None, "train"),
        P(("groups", "train"), None, None, None),
        P(("groups", "train"), None, None, None),
        P(("groups", "train")),
    )
    return jax.shard_map(
        functools.partial(on_device, mesh.shape[AXIS]),
        mesh=mesh,
        in_specs=placed,
        out_specs=P("groups", "train"),
        check_vma=False,
    )
```

```python
import functools

import jax
import jax.numpy as jnp
from jax import lax
from jax.experimental import pallas as pl
from jax.experimental.pallas import tpu as pltpu
from jax.sharding import PartitionSpec as P

R = 32
QUERIES = 4
DAMP = 0.5
TOGETHER = 2
SPREAD = 2
PIECES = 4
TERMS_VMEM = 20 * 2**20
AXIS = "train"
F32 = jnp.float32
BF16 = jnp.bfloat16


def far_stages(n, most):
    stages, bit = [], 4
    while bit < n:
        bits = min(most, (n // bit).bit_length() - 1)
        stages.append((bit, bits))
        bit <<= bits
    return stages


def swap(x, n, mask):
    return lax.ppermute(x, AXIS, [(t, t ^ mask) for t in range(n)])


def spread(block, n):
    ks = [0]
    for bit, bits in far_stages(n, SPREAD):
        masks = [bit * j for j in range(1, 1 << bits)]
        block = jnp.concatenate([block] + [swap(block, n, m) for m in masks], axis=1)
        ks = [k ^ m for m in [0] + masks for k in ks]
    return block, ks


def sum_far(total, me, n, stages):
    result = total.astype(BF16)
    for bit, bits in stages:
        if bits == 1:
            total = total + swap(result, n, bit).astype(F32)
            result = total.astype(BF16)
            continue
        place = (me // bit) % 4
        first = (place == 0) | (place == 3)
        half = total.shape[1] // 2
        low, high = total[:, :half], total[:, half:]
        mine = jnp.where(first, low, high)
        theirs = jnp.where(first, high, low).astype(BF16)
        mine = mine + swap(theirs, n, bit).astype(F32)
        mine = mine + swap(mine.astype(BF16), n, 3 * bit).astype(F32)
        mine = mine.astype(BF16)
        theirs = swap(mine, n, bit)
        result = jnp.concatenate(
            [jnp.where(first, mine, theirs), jnp.where(first, theirs, mine)], axis=1
        )
        total = result.astype(F32)
    return result


def after(x, earlier):
    return lax.optimization_barrier((x, earlier))[0] if earlier else x


def gather_near(block, n):
    across = swap(block, n, 2)
    return block, across, swap(block, n, 1), swap(across, n, 1)


def sum_near(half, me, n):
    quarter = half.shape[1] // 2
    near, away = half[:, :quarter], half[:, quarter:].astype(BF16)
    stages = far_stages(n, 2)
    if not stages or stages[0][1] == 1:
        total = near + swap(away, n, 2).astype(F32)
        block = sum_far(total, me, n, stages)
        return block, swap(block, n, 2)
    bit = stages[0][0]
    place = (me // bit) % 4
    first = (place == 0) | (place == 3)
    low, high = slice(0, quarter // 2), slice(quarter // 2, quarter)
    pick = lambda x, y: jnp.where(first, x, y)
    theirs = pick(near[:, high], near[:, low]) + swap(pick(away[:, high], away[:, low]), n, 2).astype(F32)
    mine = pick(near[:, low], near[:, high]) + swap(pick(away[:, low], away[:, high]), n, 2).astype(F32)
    mine = mine + swap(theirs.astype(BF16), n, bit).astype(F32)
    mine = mine + swap(mine.astype(BF16), n, 3 * bit).astype(F32)
    mine = sum_far(mine, me, n, stages[1:])
    theirs = swap(mine, n, bit)
    join = lambda x, y: jnp.concatenate([pick(x, y), pick(y, x)], axis=1)
    return join(mine, theirs), join(swap(mine, n, 2), swap(theirs, n, 2))


def term_kernel(n, column, first, offsets, me_ref, *refs):
    count = len(offsets)
    arrays, rest = refs[:count], refs[count:]
    basis, eig, send, keep, full, held, pair, sems, *stages, in_sems = rest
    me = me_ref[0]
    layers, _, width = held.shape
    rows = width // n
    piece = width // PIECES
    copies = {}
    for l in range(layers):
        for i, (array, stage) in enumerate(zip(arrays, stages)):
            copies[l, -1 - i] = pltpu.make_async_copy(array.at[l], stage.at[l], in_sems.at[l, i])
            copies[l, -1 - i].start()
        for p in range(PIECES):
            part = (slice(None), pl.ds(p * piece, piece))
            copies[l, p] = pltpu.make_async_copy(
                basis.at[first + l].at[part], held.at[l].at[part], sems.at[l, p]
            )
            copies[l, p].start()
    mine = me & 1
    above = (me >> 1) & 1
    for l in range(layers):
        for j, (stage, ks) in enumerate(zip(stages, offsets)):
            copies[l, -1 - j].wait()
            for i, k in enumerate(ks):
                at = pl.multiple_of((me ^ k) * rows, rows)
                full[pl.ds(at, rows), :] = stage[l, i * rows : (i + 1) * rows, :]
        coeff = [0.0, 0.0]
        split = held.shape[1] // 2
        for p in range(PIECES):
            copies[l, p].wait()
            for h in range(2):
                coeff[h] = coeff[h] + jnp.dot(
                    held[l, h * split : (h + 1) * split, p * piece : (p + 1) * piece],
                    full[p * piece : (p + 1) * piece, :],
                    preferred_element_type=F32,
                )
        coeff = jnp.concatenate(coeff, axis=0)
        scale = eig[:, column + l : column + l + 1] + DAMP
        scaled = (coeff / scale).astype(BF16).T
        term = jnp.dot(scaled, held[l], preferred_element_type=F32)
        for p in range(n // 2):
            pair[...] = term[:, 2 * p * rows : 2 * (p + 1) * rows].T
            at = pl.multiple_of(((above ^ (p & 1)) * (n // 4) + p // 2) * rows, rows)
            kept = pl.multiple_of(mine * rows, rows)
            sent = pl.multiple_of((1 - mine) * rows, rows)
            keep[l, pl.ds(at, rows), :] = pair[pl.ds(kept, rows), :].astype(BF16)
            send[l, pl.ds(at, rows), :] = pair[pl.ds(sent, rows), :].astype(BF16)


def terms(me, arrays, offsets, basis, eig, first, column, n):
    _, cols, width = basis.shape
    layers, _, q = arrays[0].shape
    vmem = pl.BlockSpec(memory_space=pltpu.VMEM)
    half = (layers, width // 2, q)
    return pl.pallas_call(
        functools.partial(term_kernel, n, column, first, offsets),
        in_specs=[pl.BlockSpec(memory_space=pltpu.SMEM)]
        + [pl.BlockSpec(memory_space=pl.ANY)] * (len(arrays) + 1)
        + [vmem],
        out_specs=[vmem, vmem],
        scratch_shapes=[
            pltpu.VMEM((width, q), BF16),
            pltpu.VMEM((layers, cols, width), BF16),
            pltpu.VMEM((2 * width // n, q), F32),
            pltpu.SemaphoreType.DMA((layers, PIECES)),
            *[pltpu.VMEM(a.shape, BF16) for a in arrays],
            pltpu.SemaphoreType.DMA((layers, len(arrays))),
        ],
        out_shape=[jax.ShapeDtypeStruct(half, BF16)] * 2,
        compiler_params=pltpu.CompilerParams(vmem_limit_bytes=TERMS_VMEM),
        cost_estimate=pl.CostEstimate(
            flops=layers * 4 * width * cols * q,
            bytes_accessed=layers * 2 * width * (cols + 2 * q),
            transcendentals=0,
        ),
        name="terms",
    )(me, *[pltpu.with_memory_space_constraint(a, pltpu.HBM) for a in arrays], pltpu.with_memory_space_constraint(basis, pltpu.HBM), eig)


def proj_kernel(n, first, me_ref, pa, pb, pc, pd, train, *rest):
    *other, out, full, held, sems = rest
    layers, tables, s, width = held.shape
    rows = width // n
    copies = []
    for l in range(layers):
        copies.append(pltpu.make_async_copy(train.at[:, first + l], held.at[l], sems.at[l]))
        copies[l].start()
    total = 0.0
    for l in range(layers):
        for quarter, mask in zip((pa, pb, pc, pd), (0, 2, 1, 3)):
            for i in range(n // 4):
                at = pl.multiple_of((4 * i + ((me_ref[0] & 3) ^ mask)) * rows, rows)
                full[pl.ds(at, rows), :] = quarter[l, i * rows : (i + 1) * rows, :]
        copies[l].wait()
        proj = jnp.dot(
            held[l].reshape(tables * s, width), full[...], preferred_element_type=F32
        )
        if other:
            product = (proj * other[0][l]).reshape(tables, s, proj.shape[1])
            total = total + jnp.sum(product, axis=1)
        else:
            out[l] = proj
    if other:
        out[...] = total


def project(me, quarters, train, first, n, other=()):
    tables, _, s, width = train.shape
    layers, _, q = quarters[0].shape
    vmem = pl.BlockSpec(memory_space=pltpu.VMEM)
    shape = (tables, q) if other else (layers, tables * s, q)
    return pl.pallas_call(
        functools.partial(proj_kernel, n, first),
        in_specs=[pl.BlockSpec(memory_space=pltpu.SMEM)]
        + [vmem] * 4
        + [pl.BlockSpec(memory_space=pltpu.HBM)]
        + [vmem] * len(other),
        out_specs=vmem,
        scratch_shapes=[
            pltpu.VMEM((width, q), BF16),
            pltpu.VMEM((layers, tables, s, width), BF16),
            pltpu.SemaphoreType.DMA((layers,)),
        ],
        out_shape=jax.ShapeDtypeStruct(shape, F32),
        compiler_params=pltpu.CompilerParams(vmem_limit_bytes=TERMS_VMEM),
        cost_estimate=pl.CostEstimate(
            flops=layers * 2 * width * tables * s * q,
            bytes_accessed=layers * 2 * width * (tables * s + q),
            transcendentals=0,
        ),
        name="project",
    )(me, *quarters, train, *other)


def on_device(
    n, q_left, q_right, left_basis, right_basis, left_eig, right_eig, train_left, train_right, seq_ids
):
    layers = q_left.shape[0]
    tables = train_left.shape[0]
    me = lax.axis_index(AXIS).astype(jnp.int32).reshape(1)
    eig = jnp.concatenate((left_eig, right_eig), axis=0).T
    sides = (
        (q_left, jnp.swapaxes(left_basis, 1, 2), train_left),
        (q_right, jnp.swapaxes(right_basis, 1, 2), train_right),
    )
    chunks = [(first, side) for first in range(0, layers, TOGETHER) for side in range(2)]
    blocks = [spread(sides[side][0][first : first + TOGETHER], n) for first, side in chunks]
    gathered = []
    for i, (block, _) in enumerate(blocks):
        across = swap(block, n, 2)
        ready = after(across, [other for other, _ in blocks[i + 1 : i + 2]])
        gathered.append((block, across, swap(block, n, 1), swap(ready, n, 1)))
    halves = []
    for i, (first, side) in enumerate(chunks):
        ks = blocks[i][1]
        offsets = [[k ^ m for k in ks] for m in (0, 2, 1, 3)]
        earlier = []
        arrays = after(gathered[i], earlier)
        send, keep = terms(me, arrays, offsets, sides[side][1], eig, first, side * layers + first, n)
        half = keep.astype(F32) + swap(send, n, 1).astype(F32)
        halves.append(sum_near(half, me[0], n))
    total, left = 0.0, ()
    for i, (first, side) in enumerate(chunks):
        block, across = halves[i]
        corner = swap(after(across, left), n, 1)
        left = (project(me, (block, across, swap(block, n, 1), corner), sides[side][2], first, n, left),)
        if side:
            total, left = total + left[0], ()
    table_scores = jnp.sum(total.reshape(tables, QUERIES, R), axis=2).T
    match = (seq_ids[None, :] == jnp.arange(tables, dtype=jnp.int32)[:, None]).astype(F32)
    return jnp.dot(table_scores, match, precision=lax.Precision.HIGHEST, preferred_element_type=F32)


def solution(mesh):
    placed = (
        P(None, "train", "groups"),
        P(None, "train", "groups"),
        P(None, None, "train"),
        P(None, None, "train"),
        P(None, "train"),
        P(None, "train"),
        P(("groups", "train"), None, None, None),
        P(("groups", "train"), None, None, None),
        P(("groups", "train")),
    )
    return jax.shard_map(
        functools.partial(on_device, mesh.shape[AXIS]),
        mesh=mesh,
        in_specs=placed,
        out_specs=P("groups", "train"),
        check_vma=False,
    )
```

```python
import functools

import jax
import jax.numpy as jnp
from jax import lax
from jax.experimental import pallas as pl
from jax.experimental.pallas import tpu as pltpu
from jax.sharding import PartitionSpec as P

R = 32
QUERIES = 4
DAMP = 0.5
TOGETHER = 2
SPREAD = 2
PIECES = 4
TERMS_VMEM = 20 * 2**20
AXIS = "train"
F32 = jnp.float32
BF16 = jnp.bfloat16


def far_stages(n, most):
    stages, bit = [], 4
    while bit < n:
        bits = min(most, (n // bit).bit_length() - 1)
        stages.append((bit, bits))
        bit <<= bits
    return stages


def swap(x, n, mask):
    return lax.ppermute(x, AXIS, [(t, t ^ mask) for t in range(n)])


def spread(block, n):
    ks = [0]
    for bit, bits in far_stages(n, SPREAD):
        masks = [bit * j for j in range(1, 1 << bits)]
        block = jnp.concatenate([block] + [swap(block, n, m) for m in masks], axis=1)
        ks = [k ^ m for m in [0] + masks for k in ks]
    return block, ks


def sum_far(total, me, n, stages):
    result = total.astype(BF16)
    for bit, bits in stages:
        if bits == 1:
            total = total + swap(result, n, bit).astype(F32)
            result = total.astype(BF16)
            continue
        place = (me // bit) % 4
        first = (place == 0) | (place == 3)
        half = total.shape[1] // 2
        low, high = total[:, :half], total[:, half:]
        mine = jnp.where(first, low, high)
        theirs = jnp.where(first, high, low).astype(BF16)
        mine = mine + swap(theirs, n, bit).astype(F32)
        mine = mine + swap(mine.astype(BF16), n, 3 * bit).astype(F32)
        mine = mine.astype(BF16)
        theirs = swap(mine, n, bit)
        result = jnp.concatenate(
            [jnp.where(first, mine, theirs), jnp.where(first, theirs, mine)], axis=1
        )
        total = result.astype(F32)
    return result


def after(x, earlier):
    return lax.optimization_barrier((x, earlier))[0] if earlier else x


def gather_near(block, n):
    across = swap(block, n, 2)
    return block, across, swap(block, n, 1), swap(across, n, 1)


def sum_near(keep, got, earlier, me, n):
    quarter = keep.shape[1] // 2
    near = keep[:, :quarter].astype(F32) + got[:, :quarter].astype(F32)
    away = (keep[:, quarter:].astype(F32) + got[:, quarter:].astype(F32)).astype(BF16)
    away = after(away, earlier)
    stages = far_stages(n, 2)
    if not stages or stages[0][1] == 1:
        total = near + swap(away, n, 2).astype(F32)
        block = sum_far(total, me, n, stages)
        return block, swap(block, n, 2), total
    bit = stages[0][0]
    place = (me // bit) % 4
    first = (place == 0) | (place == 3)
    low, high = slice(0, quarter // 2), slice(quarter // 2, quarter)
    pick = lambda x, y: jnp.where(first, x, y)
    theirs = pick(near[:, high], near[:, low]) + swap(pick(away[:, high], away[:, low]), n, 2).astype(F32)
    mine = pick(near[:, low], near[:, high]) + swap(pick(away[:, low], away[:, high]), n, 2).astype(F32)
    summed = mine
    mine = mine + swap(theirs.astype(BF16), n, bit).astype(F32)
    mine = mine + swap(mine.astype(BF16), n, 3 * bit).astype(F32)
    mine = sum_far(mine, me, n, stages[1:])
    theirs = swap(mine, n, bit)
    join = lambda x, y: jnp.concatenate([pick(x, y), pick(y, x)], axis=1)
    return join(mine, theirs), join(swap(mine, n, 2), swap(theirs, n, 2)), summed


def term_kernel(n, column, first, offsets, me_ref, *refs):
    count = len(offsets)
    arrays, rest = refs[:count], refs[count:]
    basis, eig, send, keep, full, held, pair, sems, *stages, in_sems = rest
    me = me_ref[0]
    layers, _, width = held.shape
    rows = width // n
    piece = width // PIECES
    copies = {}
    for l in range(layers):
        for i, (array, stage) in enumerate(zip(arrays, stages)):
            copies[l, -1 - i] = pltpu.make_async_copy(array.at[l], stage.at[l], in_sems.at[l, i])
            copies[l, -1 - i].start()
        for p in range(PIECES):
            part = (slice(None), pl.ds(p * piece, piece))
            copies[l, p] = pltpu.make_async_copy(
                basis.at[first + l].at[part], held.at[l].at[part], sems.at[l, p]
            )
            copies[l, p].start()
    mine = me & 1
    above = (me >> 1) & 1
    for l in range(layers):
        for j, (stage, ks) in enumerate(zip(stages, offsets)):
            copies[l, -1 - j].wait()
            for i, k in enumerate(ks):
                at = pl.multiple_of((me ^ k) * rows, rows)
                full[pl.ds(at, rows), :] = stage[l, i * rows : (i + 1) * rows, :]
        coeff = [0.0, 0.0]
        split = held.shape[1] // 2
        for p in range(PIECES):
            copies[l, p].wait()
            for h in range(2):
                coeff[h] = coeff[h] + jnp.dot(
                    held[l, h * split : (h + 1) * split, p * piece : (p + 1) * piece],
                    full[p * piece : (p + 1) * piece, :],
                    preferred_element_type=F32,
                )
        coeff = jnp.concatenate(coeff, axis=0)
        scale = eig[:, column + l : column + l + 1] + DAMP
        scaled = (coeff / scale).astype(BF16).T
        term = jnp.dot(scaled, held[l], preferred_element_type=F32)
        for p in range(n // 2):
            pair[...] = term[:, 2 * p * rows : 2 * (p + 1) * rows].T
            at = pl.multiple_of(((above ^ (p & 1)) * (n // 4) + p // 2) * rows, rows)
            kept = pl.multiple_of(mine * rows, rows)
            sent = pl.multiple_of((1 - mine) * rows, rows)
            keep[l, pl.ds(at, rows), :] = pair[pl.ds(kept, rows), :].astype(BF16)
            send[l, pl.ds(at, rows), :] = pair[pl.ds(sent, rows), :].astype(BF16)


def terms(me, arrays, offsets, basis, eig, first, column, n):
    _, cols, width = basis.shape
    layers, _, q = arrays[0].shape
    vmem = pl.BlockSpec(memory_space=pltpu.VMEM)
    half = (layers, width // 2, q)
    return pl.pallas_call(
        functools.partial(term_kernel, n, column, first, offsets),
        in_specs=[pl.BlockSpec(memory_space=pltpu.SMEM)]
        + [pl.BlockSpec(memory_space=pl.ANY)] * (len(arrays) + 1)
        + [vmem],
        out_specs=[vmem, vmem],
        scratch_shapes=[
            pltpu.VMEM((width, q), BF16),
            pltpu.VMEM((layers, cols, width), BF16),
            pltpu.VMEM((2 * width // n, q), F32),
            pltpu.SemaphoreType.DMA((layers, PIECES)),
            *[pltpu.VMEM(a.shape, BF16) for a in arrays],
            pltpu.SemaphoreType.DMA((layers, len(arrays))),
        ],
        out_shape=[jax.ShapeDtypeStruct(half, BF16)] * 2,
        compiler_params=pltpu.CompilerParams(vmem_limit_bytes=TERMS_VMEM),
        cost_estimate=pl.CostEstimate(
            flops=layers * 4 * width * cols * q,
            bytes_accessed=layers * 2 * width * (cols + 2 * q),
            transcendentals=0,
        ),
        name="terms",
    )(me, *[pltpu.with_memory_space_constraint(a, pltpu.HBM) for a in arrays], pltpu.with_memory_space_constraint(basis, pltpu.HBM), eig)


def proj_kernel(n, first, me_ref, pa, pb, pc, pd, train, *rest):
    *other, out, full, held, sems = rest
    layers, tables, s, width = held.shape
    rows = width // n
    copies = []
    for l in range(layers):
        copies.append(pltpu.make_async_copy(train.at[:, first + l], held.at[l], sems.at[l]))
        copies[l].start()
    total = 0.0
    for l in range(layers):
        for quarter, mask in zip((pa, pb, pc, pd), (0, 2, 1, 3)):
            for i in range(n // 4):
                at = pl.multiple_of((4 * i + ((me_ref[0] & 3) ^ mask)) * rows, rows)
                full[pl.ds(at, rows), :] = quarter[l, i * rows : (i + 1) * rows, :]
        copies[l].wait()
        proj = jnp.dot(
            held[l].reshape(tables * s, width), full[...], preferred_element_type=F32
        )
        if other:
            product = (proj * other[0][l]).reshape(tables, s, proj.shape[1])
            total = total + jnp.sum(product, axis=1)
        else:
            out[l] = proj
    if other:
        out[...] = total


def project(me, quarters, train, first, n, other=()):
    tables, _, s, width = train.shape
    layers, _, q = quarters[0].shape
    vmem = pl.BlockSpec(memory_space=pltpu.VMEM)
    shape = (tables, q) if other else (layers, tables * s, q)
    return pl.pallas_call(
        functools.partial(proj_kernel, n, first),
        in_specs=[pl.BlockSpec(memory_space=pltpu.SMEM)]
        + [vmem] * 4
        + [pl.BlockSpec(memory_space=pltpu.HBM)]
        + [vmem] * len(other),
        out_specs=vmem,
        scratch_shapes=[
            pltpu.VMEM((width, q), BF16),
            pltpu.VMEM((layers, tables, s, width), BF16),
            pltpu.SemaphoreType.DMA((layers,)),
        ],
        out_shape=jax.ShapeDtypeStruct(shape, F32),
        compiler_params=pltpu.CompilerParams(vmem_limit_bytes=TERMS_VMEM),
        cost_estimate=pl.CostEstimate(
            flops=layers * 2 * width * tables * s * q,
            bytes_accessed=layers * 2 * width * (tables * s + q),
            transcendentals=0,
        ),
        name="project",
    )(me, *quarters, train, *other)


def on_device(
    n, q_left, q_right, left_basis, right_basis, left_eig, right_eig, train_left, train_right, seq_ids
):
    layers = q_left.shape[0]
    tables = train_left.shape[0]
    me = lax.axis_index(AXIS).astype(jnp.int32).reshape(1)
    eig = jnp.concatenate((left_eig, right_eig), axis=0).T
    sides = (
        (q_left, jnp.swapaxes(left_basis, 1, 2), train_left),
        (q_right, jnp.swapaxes(right_basis, 1, 2), train_right),
    )
    chunks = [(first, side) for first in range(0, layers, TOGETHER) for side in range(2)]
    blocks = [spread(sides[side][0][first : first + TOGETHER], n) for first, side in chunks]
    gathered = []
    for i, (block, _) in enumerate(blocks):
        across = swap(block, n, 2)
        ready = after(across, [other for other, _ in blocks[i + 1 : i + 2]])
        gathered.append((block, across, swap(block, n, 1), swap(ready, n, 1)))
    halves = []
    for i, (first, side) in enumerate(chunks):
        ks = blocks[i][1]
        offsets = [[k ^ m for k in ks] for m in (0, 2, 1, 3)]
        earlier = []
        arrays = after(gathered[i], earlier)
        send, keep = terms(me, arrays, offsets, sides[side][1], eig, first, side * layers + first, n)
        earlier = [done[2] for done in halves[-1:]]
        halves.append(sum_near(keep, swap(send, n, 1), earlier, me[0], n))
    total, left = 0.0, ()
    for i, (first, side) in enumerate(chunks):
        block, across, _ = halves[i]
        corner = swap(after(across, left), n, 1)
        left = (project(me, (block, across, swap(block, n, 1), corner), sides[side][2], first, n, left),)
        if side:
            total, left = total + left[0], ()
    table_scores = jnp.sum(total.reshape(tables, QUERIES, R), axis=2).T
    match = (seq_ids[None, :] == jnp.arange(tables, dtype=jnp.int32)[:, None]).astype(F32)
    return jnp.dot(table_scores, match, precision=lax.Precision.HIGHEST, preferred_element_type=F32)


def solution(mesh):
    placed = (
        P(None, "train", "groups"),
        P(None, "train", "groups"),
        P(None, None, "train"),
        P(None, None, "train"),
        P(None, "train"),
        P(None, "train"),
        P(("groups", "train"), None, None, None),
        P(("groups", "train"), None, None, None),
        P(("groups", "train")),
    )
    return jax.shard_map(
        functools.partial(on_device, mesh.shape[AXIS]),
        mesh=mesh,
        in_specs=placed,
        out_specs=P("groups", "train"),
        check_vma=False,
    )
```
